256 devices in a mesh: blk: 32 (over z_hi, x, core), uly: 8 (over z_lo, y).
Axes of the slice: x: 4, y: 4, z: 8 (z_hi: 4, z_lo: 2; z = z_hi * 2 + z_lo), core: 2. Of those that a mesh axis runs over, the one named last changes fastest.
Arguments:
- queries: bfloat16 [32768, 4096], P(('blk', 'uly')), may hold values from -14 to 14
- keys: bfloat16 [32768, 512], P(('blk', 'uly')), may hold values from -6 to 6
- values: bfloat16 [32768, 512], P(('blk', 'uly')), may hold values from -6 to 6
- head_grads: bfloat16 [32768, 4096], P(('blk', 'uly')), may hold values from -6 to 6
- cotangent: bfloat16 [32768, 4096], P(('blk', 'uly')), may hold values from -24 to 24
- old_logprobs: float32 [32768], P(('blk', 'uly')), may hold values from -4 to 0
- new_logprobs: float32 [32768], P(('blk', 'uly')), may hold values from -4 to 0
- doc_lengths: int32 [128], replicated, may hold values from 1 to 512, 32768 in all
Outputs:
- grad_queries: float32 [32768, 4096], P(('blk', 'uly'))
- key_gradient: float32 [32768, 512], P(('blk', 'uly'))
- value_gradient: float32 [32768, 512], P(('blk', 'uly'))
- grad_out_weight: float32 [4096, 4096], P('uly', 'blk')
The draws below stay inside these ranges and needn't reach their ends.
Inputs may be any that keep to these rules, and one draw needn't show every extreme that they name: `doc_lengths`: the lengths sum to 32768.
All inputs are finite; a program needn't handle non-finite values.
Results may differ from the reference program's by a relative error of at most 0.035.
Values may be sent and summed in bfloat16 or wider, within the bound.
No kernel may reach another device: no remote copies, remote signals or barrier semaphores. Data moves between devices by JAX's collectives and lax.ppermute only.
A program may use at most 128 MiB of HBM per device.

```python
import math
import jax
import jax.numpy as jnp
import numpy as np
from jax import lax

QUERY_HEAD_COUNT = 32
KEY_VALUE_HEADS = 4
HEAD_WIDTH = 128
D_OUT = 4096
SEQ_DEV = 128
LONGEST = 512
PACKED_TOKENS = 32768
DOCS = 128
N_ULY = 8


def common_rows(key):
    starting_keys = jnp.clip(jax.random.normal(key, (PACKED_TOKENS, KEY_VALUE_HEADS, HEAD_WIDTH), jnp.float32), -6.0, 6.0)
    return starting_keys


def draw_keys(key, part):
    starting_keys = common_rows(key)
    return starting_keys.reshape(PACKED_TOKENS, KEY_VALUE_HEADS * HEAD_WIDTH).astype(jnp.bfloat16)


def draw_queries(key, part):
    key = jax.random.fold_in(key, 5)
    drawn = jnp.clip(jax.random.normal(key, (PACKED_TOKENS, QUERY_HEAD_COUNT, HEAD_WIDTH), jnp.float32), -6.0, 6.0)
    return drawn.reshape(PACKED_TOKENS, QUERY_HEAD_COUNT * HEAD_WIDTH).astype(jnp.bfloat16)


def with_spikes(result, stream_key, source, target, parts, factor):
    owner, partner = [(jnp.arange(result.shape[position]) // (result.shape[position] // parts)).reshape([-1 if axis == position else 1 for axis in range(result.ndim)]) for position in (source, target)]
    chosen = jax.random.permutation(stream_key, parts)[partner]
    strong = (owner == chosen) | (owner == (partner + parts // 2) % parts)
    return jnp.where(strong, factor * result, result)


def steps_of(rng, extent, shards, least, high):
    def one(axis_at, parts):
        steps = jax.random.uniform(jax.random.fold_in(jax.random.fold_in(rng, 6), axis_at), (parts,), jnp.float32, least / len(shards), high / len(shards))
        return jnp.repeat(jnp.exp(steps), extent[axis_at] // parts).reshape((-1,) + (1,) * (len(extent) - axis_at - 1))

    gain = one(*shards[0])
    for cut in shards[1:]:
        gain = gain * one(*cut)
    return gain


def profile(number_of, total, limit, skew):
    weights = [(1 << 20) // math.isqrt(rank ** skew) + 1 for rank in range(2, number_of + 1)]
    surplus, holding = total - limit - (number_of - 1), [1] * (number_of - 1)
    while surplus > 0:
        free = [i for i in range(number_of - 1) if holding[i] < limit]
        whole, left = sum([weights[i] for i in free]), surplus
        for i in free:
            extra = min(limit - holding[i], max(1, left * weights[i] // whole), surplus)
            holding[i] = holding[i] + extra
            surplus = surplus - extra
    return np.array([limit] + holding)


def uneven_parts(stream_key, count, total, most, skew):
    if count == 2:
        one = jax.random.randint(stream_key, (), max(1, total - most), min(most, total - 1) + 1)
        return jnp.stack([one, total - one])
    sizes = jnp.asarray(profile(count, total, most, skew), jnp.int32)
    twos = (count - 1) // 2
    giver, taker = sizes[1:1 + 2 * twos:2], sizes[2:2 + 2 * twos:2]
    slack = jnp.minimum(giver - 1, most - taker)
    moved = jax.random.randint(jax.random.fold_in(stream_key, 1), (twos,), 0, 1 << 20) % (slack + 1)
    sizes = sizes.at[1:1 + 2 * twos:2].set(giver - moved).at[2:2 + 2 * twos:2].set(taker + moved)
    return sizes[jax.random.permutation(jax.random.fold_in(stream_key, 2), count)]


def bell_draw(stream_key, shape, spread, reach, cuts=(), held_as=jnp.bfloat16):
    values = spread * jax.random.normal(stream_key, shape, jnp.float32)
    if cuts:
        values = values * steps_of(stream_key, shape, cuts, -0.22, 0.18)
    return jnp.clip(values, -reach, reach).astype(held_as)


def heavy_noise(stream_key, extent, deviation, most, split, heavy, kind=jnp.bfloat16):
    result = deviation * jax.random.normal(stream_key, extent, jnp.float32)
    if split:
        result = result * steps_of(stream_key, extent, split, -0.22, 0.18)
    return jnp.clip(with_spikes(result, jax.random.fold_in(stream_key, 3), *heavy), -most, most).astype(kind)


def setup_inputs(seed: int = 0) -> dict:
    key_list = jax.random.split(jax.random.key(seed), 9)
    queries = draw_queries(jax.random.fold_in(key_list[8], 71), 0)
    keys = draw_keys(jax.random.fold_in(key_list[8], 71), 0)
    values = bell_draw(key_list[2], (PACKED_TOKENS, KEY_VALUE_HEADS * HEAD_WIDTH), 1.0, 6.0, ((0, 256),))
    head_grads = bell_draw(key_list[3], (PACKED_TOKENS, QUERY_HEAD_COUNT * HEAD_WIDTH), 1.0, 6.0, ((0, 256),))
    cotangent = heavy_noise(key_list[4], (PACKED_TOKENS, D_OUT), 1.0, 24.0, ((0, 256),), (0, 1, 256, 6.0))
    old_logprobs = jnp.clip(-4.0 + 4.0 * jax.random.uniform(key_list[5], (PACKED_TOKENS,), jnp.float32) ** steps_of(key_list[5], (PACKED_TOKENS,), ((0, 256),), -0.2, 0.2), -4.0, 0.0)
    new_logprobs = jnp.clip(-4.0 + 4.0 * jax.random.uniform(key_list[6], (PACKED_TOKENS,), jnp.float32) ** steps_of(key_list[6], (PACKED_TOKENS,), ((0, 256),), -0.2, 0.2), -4.0, 0.0)
    doc_lengths = uneven_parts(key_list[7], DOCS, PACKED_TOKENS, LONGEST, 2).astype(jnp.int32)
    return {"queries": queries, "keys": keys, "values": values, "head_grads": head_grads, "cotangent": cotangent, "old_logprobs": old_logprobs, "new_logprobs": new_logprobs, "doc_lengths": doc_lengths}


clip_top = 2.0
neg_fill = -1e+30

def doc_starts(positions, lengths):
    ends = jnp.cumsum(lengths).astype(jnp.int32)
    before = jnp.where(ends[None, :] <= positions[:, None], lengths[None, :], 0)
    return lax.optimization_barrier(jnp.sum(before, axis=1)).astype(jnp.int32)

def reference(queries, keys, values, head_grads, cotangent, old_logprobs, new_logprobs, doc_lengths):
    score_scale = 1.0 / math.sqrt(HEAD_WIDTH)
    group_width = QUERY_HEAD_COUNT // KEY_VALUE_HEADS
    block_rows = min(PACKED_TOKENS, 1024)
    longest = LONGEST
    ratios = jnp.minimum(jnp.exp(new_logprobs - old_logprobs), clip_top)
    weighted = (ratios[:, None] * cotangent.astype(jnp.float32)).astype(jnp.bfloat16)
    grad_out = (ratios[:, None] * head_grads.astype(jnp.float32)).astype(jnp.bfloat16)
    positions = jnp.arange(PACKED_TOKENS, dtype=jnp.int32)
    first_rows = doc_starts(positions, doc_lengths)
    query_heads = queries.reshape(PACKED_TOKENS, QUERY_HEAD_COUNT, HEAD_WIDTH).transpose(1, 0, 2)
    heads_of_keys = keys.reshape(PACKED_TOKENS, KEY_VALUE_HEADS, HEAD_WIDTH).transpose(1, 0, 2)
    heads_of_values = values.reshape(PACKED_TOKENS, KEY_VALUE_HEADS, HEAD_WIDTH).transpose(1, 0, 2)
    grad_heads = grad_out.reshape(PACKED_TOKENS, QUERY_HEAD_COUNT, HEAD_WIDTH).transpose(1, 0, 2)

    def one_head(packed):
        query_head, grad_head, head_number = packed
        key_head = lax.dynamic_index_in_dim(heads_of_keys, head_number // group_width, 0, keepdims=False)
        value_head = lax.dynamic_index_in_dim(heads_of_values, head_number // group_width, 0, keepdims=False)
        outputs = []
        query_grads = []
        key_grad = jnp.zeros((PACKED_TOKENS, HEAD_WIDTH), jnp.float32)
        value_grad = jnp.zeros((PACKED_TOKENS, HEAD_WIDTH), jnp.float32)
        for block_number in range(PACKED_TOKENS // block_rows):
            low_row = block_number * block_rows
            high_row = low_row + block_rows
            key_low = max(0, low_row - longest)
            query_block = query_head[low_row:high_row]
            grad_block = grad_head[low_row:high_row]
            key_block = key_head[key_low:high_row]
            value_block = value_head[key_low:high_row]
            allowed = (positions[None, key_low:high_row] <= positions[low_row:high_row, None]) & (positions[None, key_low:high_row] >= first_rows[low_row:high_row, None])
            scores = jnp.dot(query_block, key_block.T, preferred_element_type=jnp.float32) * score_scale
            scores = jnp.where(allowed, scores, neg_fill)
            row_max = lax.optimization_barrier(jnp.max(scores, axis=1, keepdims=True))
            row_total = lax.optimization_barrier(jnp.sum(jnp.where(allowed, jnp.exp(scores - row_max), 0.0), axis=1, keepdims=True))
            log_total = row_max + jnp.log(row_total)
            probability = jnp.where(allowed, jnp.exp(scores - log_total), 0.0)
            out_block = jnp.dot(probability.astype(jnp.bfloat16), value_block, preferred_element_type=jnp.float32).astype(jnp.bfloat16)
            delta = lax.optimization_barrier(jnp.sum(grad_block.astype(jnp.float32) * out_block.astype(jnp.float32), axis=1, keepdims=True))
            grad_probs = jnp.dot(grad_block, value_block.T, preferred_element_type=jnp.float32)
            grad_scores = probability * (grad_probs - delta)
            probs_low = probability.astype(jnp.bfloat16)
            scores_low = grad_scores.astype(jnp.bfloat16)
            value_grad = value_grad.at[key_low:high_row].add(jnp.dot(probs_low.T, grad_block, preferred_element_type=jnp.float32))
            key_grad = key_grad.at[key_low:high_row].add(score_scale * jnp.dot(scores_low.T, query_block, preferred_element_type=jnp.float32))
            query_grads.append(score_scale * jnp.dot(scores_low, key_block, preferred_element_type=jnp.float32))
            outputs.append(out_block)
        return (jnp.concatenate(outputs, axis=0), jnp.concatenate(query_grads, axis=0), key_grad, value_grad)
    head_numbers = jnp.arange(QUERY_HEAD_COUNT, dtype=jnp.int32)
    out_all, query_all, every_key, every_value = lax.map(one_head, (query_heads, grad_heads, head_numbers))
    grad_queries = query_all.transpose(1, 0, 2).reshape(PACKED_TOKENS, QUERY_HEAD_COUNT * HEAD_WIDTH)
    key_gradient = every_key.reshape(KEY_VALUE_HEADS, group_width, PACKED_TOKENS, HEAD_WIDTH).sum(axis=1).transpose(1, 0, 2).reshape(PACKED_TOKENS, KEY_VALUE_HEADS * HEAD_WIDTH)
    value_gradient = every_value.reshape(KEY_VALUE_HEADS, group_width, PACKED_TOKENS, HEAD_WIDTH).sum(axis=1).transpose(1, 0, 2).reshape(PACKED_TOKENS, KEY_VALUE_HEADS * HEAD_WIDTH)
    out_flat = out_all.transpose(1, 0, 2).reshape(PACKED_TOKENS, QUERY_HEAD_COUNT * HEAD_WIDTH)
    block_count = PACKED_TOKENS // (SEQ_DEV * N_ULY)
    out_blocks = out_flat.reshape(block_count, PACKED_TOKENS // block_count, QUERY_HEAD_COUNT * HEAD_WIDTH)
    weight_blocks = weighted.reshape(block_count, PACKED_TOKENS // block_count, D_OUT)

    def add_part(running, item):
        out_block, weight_block = item
        partial_sum = jnp.dot(out_block.T, weight_block, preferred_element_type=jnp.float32)
        partial_sum = lax.optimization_barrier(partial_sum.astype(jnp.bfloat16)).astype(jnp.float32)
        return (running + partial_sum, None)
    grad_out_weight, _ = lax.scan(add_part, jnp.zeros((QUERY_HEAD_COUNT * HEAD_WIDTH, D_OUT), jnp.float32), (out_blocks, weight_blocks))
    return (grad_queries, key_gradient, value_gradient, grad_out_weight)
```

```python
import math

import jax
import jax.numpy as jnp
from jax import lax
from jax.experimental import pallas as pl
from jax.experimental.pallas import tpu as pltpu
from jax.sharding import Mesh, PartitionSpec as P

HEAD = 128
TOKENS = 128
BACK = 4
SPAN = (BACK + 1) * TOKENS
KV_HEADS = 4
GROUP = 8
CLIP = 2.0
NEG = -1e30
SCALE = 1.0 / math.sqrt(HEAD)
LOG2E = math.log2(math.e)
FLAT = ("zh", "x", "core", "zl", "y")
BF = jnp.bfloat16
F32 = jnp.float32

NT = (((1,), (1,)), ((), ()))


def dot(a, b):
    return jnp.dot(a, b, preferred_element_type=F32)


def dot_nt(a, b):
    return lax.dot_general(a, b, NT, preferred_element_type=F32)


def mask_bias(here, lengths):
    row = lax.broadcasted_iota(jnp.int32, (TOKENS, TOKENS), 0)
    col = lax.broadcasted_iota(jnp.int32, (TOKENS, TOKENS), 1)
    lens = jnp.broadcast_to(lengths.astype(F32), (TOKENS, TOKENS))
    ends = jnp.sum(jnp.where(col <= row, lens, 0.0), axis=1, keepdims=True)
    lens_col = jnp.sum(jnp.where(col == row, lens, 0.0), axis=1, keepdims=True)
    base = here * TOKENS
    pos = (base + col).astype(F32)
    first = jnp.sum(jnp.where(ends <= pos, lens_col, 0.0), axis=0, keepdims=True)
    first = first.astype(jnp.int32)
    key = base - BACK * TOKENS + lax.broadcasted_iota(jnp.int32, (SPAN, TOKENS), 0)
    query = base + lax.broadcasted_iota(jnp.int32, (SPAN, TOKENS), 1)
    seen = (key <= query) & (key >= first)
    return jnp.where(seen, 0.0, NEG)


def scores_of(keys, q_pair, bias):
    return dot_nt(keys, q_pair) * (SCALE * LOG2E) + bias


def pair_rows(ref_or_val, pair):
    a = ref_or_val[:, (2 * pair) * HEAD : (2 * pair + 1) * HEAD]
    b = ref_or_val[:, (2 * pair + 1) * HEAD : (2 * pair + 2) * HEAD]
    return jnp.concatenate([a, b], axis=0)


def forward_kernel(here_ref, len_ref, q_ref, *refs):
    kv_refs, (out_ref, log_ref, bias_ref) = refs[: BACK + 1], refs[BACK + 1 :]

    @pl.when(pl.program_id(0) == 0)
    def _():
        bias_ref[...] = mask_bias(here_ref[0], len_ref[...])

    keys = jnp.concatenate([r[0] for r in kv_refs], axis=0)
    values_t = jnp.concatenate([r[1] for r in kv_refs], axis=0).T
    bias = jnp.concatenate([bias_ref[...]] * 2, axis=1)
    for pair in range(GROUP // 2):
        s = scores_of(keys, pair_rows(q_ref, pair), bias)
        top = jnp.max(s, axis=0, keepdims=True)
        p = jnp.exp2(s - top)
        total = jnp.sum(p, axis=0, keepdims=True)
        out_t = (dot(values_t, p.astype(BF)) / total).astype(BF)
        log_total = top + jnp.log2(total)
        for i in range(2):
            h = 2 * pair + i
            out_ref[h * HEAD : (h + 1) * HEAD, :] = out_t[:, i * TOKENS : (i + 1) * TOKENS]
            log_ref[0, h : h + 1, :] = log_total[:, i * TOKENS : (i + 1) * TOKENS]


def column_of(row):
    r = lax.broadcasted_iota(jnp.int32, (TOKENS, TOKENS), 0)
    c = lax.broadcasted_iota(jnp.int32, (TOKENS, TOKENS), 1)
    return jnp.sum(jnp.where(r == c, jnp.broadcast_to(row, (TOKENS, TOKENS)), 0.0), axis=1, keepdims=True)


def ratio_column(old_ref, new_ref):
    return column_of(jnp.minimum(jnp.exp(new_ref[...] - old_ref[...]), CLIP))


def backward_kernel(here_ref, len_ref, old_ref, new_ref, q_ref, g_ref, log_ref, *refs):
    kv_refs = refs[: BACK + 1]
    dq_ref, own_ref = refs[BACK + 1 : BACK + 3]
    back_refs = refs[BACK + 3 : 2 * BACK + 3]
    bias_ref, ratio_ref = refs[2 * BACK + 3 :]

    @pl.when(pl.program_id(0) == 0)
    def _():
        bias_ref[...] = mask_bias(here_ref[0], len_ref[...])
        ratio_ref[...] = jnp.broadcast_to(ratio_column(old_ref, new_ref), (TOKENS, HEAD))

    keys = jnp.concatenate([r[0] for r in kv_refs], axis=0)
    values = jnp.concatenate([r[1] for r in kv_refs], axis=0)
    keys_t = keys.T
    bias = jnp.concatenate([bias_ref[...]] * 2, axis=1)
    ratio = jnp.concatenate([ratio_ref[...]] * 2, axis=0)
    dk = jnp.zeros((SPAN, HEAD), F32)
    dv = jnp.zeros((SPAN, HEAD), F32)
    for pair in range(GROUP // 2):
        q = pair_rows(q_ref, pair)
        grad = (pair_rows(g_ref, pair).astype(F32) * ratio).astype(BF)
        logs = jnp.concatenate([log_ref[0, 2 * pair : 2 * pair + 1, :], log_ref[0, 2 * pair + 1 : 2 * pair + 2, :]], axis=1)
        p = jnp.exp2(scores_of(keys, q, bias) - logs)
        dp = dot_nt(values, grad)
        delta = jnp.sum(p * dp, axis=0, keepdims=True)
        ds = (p * (dp - delta)).astype(BF)
        dv = dv + dot(p.astype(BF), grad)
        dk = dk + dot(ds, q)
        dq_t = dot(keys_t, ds) * SCALE
        for i in range(2):
            h = 2 * pair + i
            dq_ref[:, h * HEAD : (h + 1) * HEAD] = dq_t[:, i * TOKENS : (i + 1) * TOKENS].T
    dk = dk * SCALE
    own_ref[0] = dk[BACK * TOKENS :]
    own_ref[1] = dv[BACK * TOKENS :]
    for j, ref in enumerate(back_refs):
        at = (BACK - 1 - j) * TOKENS
        ref[0] = dk[at : at + TOKENS].astype(BF)
        ref[1] = dv[at : at + TOKENS].astype(BF)


def params(mib):
    return pltpu.CompilerParams(vmem_limit_bytes=mib * 2**20)


KV_SPEC = pl.BlockSpec((2, TOKENS, HEAD), lambda g, *_: (0, 0, g))
ROW_SPEC = pl.BlockSpec((1, TOKENS), lambda g, *_: (0, 0))
Q_SPEC = pl.BlockSpec((TOKENS, GROUP * HEAD), lambda g, *_: (0, g))
LOG_SPEC = pl.BlockSpec((1, GROUP, TOKENS), lambda g, *_: (g, 0, 0))


def attention_forward(here, lengths, q, kvs):
    rows = q.shape[1]
    return pl.pallas_call(
        forward_kernel,
        grid_spec=pltpu.PrefetchScalarGridSpec(
            num_scalar_prefetch=1,
            grid=(KV_HEADS,),
            in_specs=[ROW_SPEC, Q_SPEC] + [KV_SPEC] * (BACK + 1),
            out_specs=[pl.BlockSpec((GROUP * HEAD, TOKENS), lambda g, *_: (g, 0)), LOG_SPEC],
            scratch_shapes=[pltpu.VMEM((SPAN, TOKENS), F32)],
        ),
        out_shape=[
            jax.ShapeDtypeStruct((rows, TOKENS), BF),
            jax.ShapeDtypeStruct((KV_HEADS, GROUP, TOKENS), F32),
        ],
        compiler_params=params(32),
        cost_estimate=pl.CostEstimate(flops=2 * 2 * 32 * 128 * 640 * 128, bytes_accessed=2**22, transcendentals=32 * 128 * 640),
        name="attention_forward",
    )(here, lengths, q, *kvs)


def attention_backward(here, lengths, old, new, q, g, logs, kvs):
    kv_shape = (2, TOKENS, KV_HEADS * HEAD)
    return pl.pallas_call(
        backward_kernel,
        grid_spec=pltpu.PrefetchScalarGridSpec(
            num_scalar_prefetch=1,
            grid=(KV_HEADS,),
            in_specs=[ROW_SPEC, ROW_SPEC, ROW_SPEC, Q_SPEC, Q_SPEC, LOG_SPEC] + [KV_SPEC] * (BACK + 1),
            out_specs=[Q_SPEC, KV_SPEC] + [KV_SPEC] * BACK,
            scratch_shapes=[pltpu.VMEM((SPAN, TOKENS), F32), pltpu.VMEM((TOKENS, HEAD), F32)],
        ),
        out_shape=[
            jax.ShapeDtypeStruct(q.shape, F32),
            jax.ShapeDtypeStruct(kv_shape, F32),
        ]
        + [jax.ShapeDtypeStruct(kv_shape, BF)] * BACK,
        compiler_params=params(32),
        cost_estimate=pl.CostEstimate(flops=5 * 2 * 32 * 128 * 640 * 128, bytes_accessed=2**23, transcendentals=32 * 128 * 640),
        name="attention_backward",
    )(here, lengths, old, new, q, g, logs, *kvs)


def along_tokens(v, by):
    count = 1
    for axis in FLAT:
        count *= lax.axis_size(axis)
    return lax.ppermute(v, FLAT, [(i, i + by) for i in range(count) if 0 <= i + by < count])


def turn(v, axis, by):
    size = lax.axis_size(axis)
    return lax.ppermute(v, axis, [(i, (i + by) % size) for i in range(size)])


def shards(queries, keys, values, head_grads, cotangent, old, new, doc_lengths):
    here = lax.axis_index(FLAT).astype(jnp.int32).reshape(1)
    lengths = doc_lengths.reshape(1, -1)
    old = old.reshape(1, -1)
    new = new.reshape(1, -1)
    core = lax.axis_index("core")

    kv = jnp.stack([keys, values])
    kvs = [along_tokens(kv, by) for by in range(BACK, 0, -1)] + [kv]

    ratios = jnp.minimum(jnp.exp(new - old), CLIP).reshape(-1, 1)
    weighted = (ratios * cotangent.astype(F32)).astype(BF)
    halves = weighted.reshape(TOKENS, 4, 4, 2, 128).transpose(3, 0, 1, 2, 4).reshape(2, TOKENS, -1)
    keep = lax.dynamic_index_in_dim(halves, core, 0, keepdims=False)
    send = lax.dynamic_index_in_dim(halves, 1 - core, 0, keepdims=False)
    mine = jnp.concatenate([keep, turn(send, "core", 1)], axis=0)
    w_all = lax.all_gather(mine, "y", axis=0, tiled=False)

    out_t, logs = attention_forward(here, lengths, queries, kvs)
    parts = lax.all_to_all(out_t.reshape(2, 4, 512, TOKENS), "y", split_axis=1, concat_axis=1, tiled=True)
    other = turn(parts, "core", 1)
    o_all = jnp.stack([parts, other], axis=2)
    part = jnp.einsum("zycrt,yctn->zrn", o_all, w_all.reshape(4, 2, TOKENS, -1), preferred_element_type=F32).astype(BF)
    part = part.reshape(2, 512, 4, 4, 128).transpose(3, 2, 0, 1, 4)
    part = lax.psum_scatter(part, "x", scatter_dimension=0, tiled=False)
    part = part.reshape(8, 512, 128)
    grad_weight = lax.psum_scatter(part, ("zh", "zl"), scatter_dimension=0, tiled=False).astype(F32)

    dq, own, *backs = attention_backward(here, lengths, old, new, queries, head_grads, logs, kvs)
    home = [along_tokens(b, -(j + 1)).astype(F32) for j, b in enumerate(backs)]
    dkv = own + sum(home)
    return dq, dkv[0], dkv[1], grad_weight


def solution(mesh):
    mesh = Mesh(mesh.devices.reshape(4, 4, 2, 2, 4), FLAT)
    tokens = P(FLAT, None)
    return jax.shard_map(
        shards,
        mesh=mesh,
        in_specs=(tokens, tokens, tokens, tokens, tokens, P(FLAT), P(FLAT), P()),
        out_specs=(tokens, tokens, tokens, P(("zl", "y"), ("zh", "x", "core"))),
        check_vma=False,
    )
```

```python
import itertools
import math

import jax
import jax.numpy as jnp
from jax import lax
from jax.experimental import pallas as pl
from jax.experimental.pallas import tpu as pltpu
from jax.sharding import Mesh, PartitionSpec as P

HEAD = 128
TOKENS = 128
BACK = 4
SPAN = (BACK + 1) * TOKENS
KV_HEADS = 4
GROUP = 8
ZH, ZL, RING = 4, 2, 4
ROWS = 1024
CLIP = 2.0
NEG = -1e30
SCALE = 1.0 / math.sqrt(HEAD)
LOG2E = math.log2(math.e)
FLAT = ("zh", "x", "core", "zl", "y")
BF = jnp.bfloat16
F32 = jnp.float32

NT = (((1,), (1,)), ((), ()))


def dot(a, b):
    return jnp.dot(a, b, preferred_element_type=F32)


def dot_nt(a, b):
    return lax.dot_general(a, b, NT, preferred_element_type=F32)


def mask_bias(here, lengths):
    row = lax.broadcasted_iota(jnp.int32, (TOKENS, TOKENS), 0)
    col = lax.broadcasted_iota(jnp.int32, (TOKENS, TOKENS), 1)
    lens = jnp.broadcast_to(lengths.astype(F32), (TOKENS, TOKENS))
    ends = jnp.sum(jnp.where(col <= row, lens, 0.0), axis=1, keepdims=True)
    lens_col = jnp.sum(jnp.where(col == row, lens, 0.0), axis=1, keepdims=True)
    base = here * TOKENS
    pos = (base + col).astype(F32)
    first = jnp.sum(jnp.where(ends <= pos, lens_col, 0.0), axis=0, keepdims=True)
    first = first.astype(jnp.int32)
    key = base - BACK * TOKENS + lax.broadcasted_iota(jnp.int32, (SPAN, TOKENS), 0)
    query = base + lax.broadcasted_iota(jnp.int32, (SPAN, TOKENS), 1)
    seen = (key <= query) & (key >= first)
    return jnp.where(seen, 0.0, NEG)


def scores_of(keys, q_pair, bias):
    return dot_nt(keys, q_pair) * (SCALE * LOG2E) + bias


def pair_rows(ref_or_val, pair):
    a = ref_or_val[:, (2 * pair) * HEAD : (2 * pair + 1) * HEAD]
    b = ref_or_val[:, (2 * pair + 1) * HEAD : (2 * pair + 2) * HEAD]
    return jnp.concatenate([a, b], axis=0)


def forward_kernel(here_ref, len_ref, q_ref, *refs):
    kv_refs, (out_ref, log_ref, bias_ref) = refs[: BACK + 1], refs[BACK + 1 :]

    @pl.when(pl.program_id(0) == 0)
    def _():
        bias_ref[...] = mask_bias(here_ref[0], len_ref[...])

    keys = jnp.concatenate([r[0] for r in kv_refs], axis=0)
    values_t = jnp.concatenate([r[1] for r in kv_refs], axis=0).T
    bias = jnp.concatenate([bias_ref[...]] * 2, axis=1)
    for pair in range(GROUP // 2):
        s = scores_of(keys, pair_rows(q_ref, pair), bias)
        top = jnp.max(s, axis=0, keepdims=True)
        p = jnp.exp2(s - top)
        total = jnp.sum(p, axis=0, keepdims=True)
        out_t = (dot(values_t, p.astype(BF)) / total).astype(BF)
        log_total = top + jnp.log2(total)
        for i in range(2):
            h = 2 * pair + i
            out_ref[h * HEAD : (h + 1) * HEAD, :] = out_t[:, i * TOKENS : (i + 1) * TOKENS]
            log_ref[0, h : h + 1, :] = log_total[:, i * TOKENS : (i + 1) * TOKENS]


def column_of(row):
    r = lax.broadcasted_iota(jnp.int32, (TOKENS, TOKENS), 0)
    c = lax.broadcasted_iota(jnp.int32, (TOKENS, TOKENS), 1)
    return jnp.sum(jnp.where(r == c, jnp.broadcast_to(row, (TOKENS, TOKENS)), 0.0), axis=1, keepdims=True)


def ratio_column(old_ref, new_ref):
    return column_of(jnp.minimum(jnp.exp(new_ref[...] - old_ref[...]), CLIP))


def backward_kernel(here_ref, len_ref, old_ref, new_ref, q_ref, g_ref, log_ref, *refs):
    kv_refs = refs[: BACK + 1]
    dq_ref, own_ref = refs[BACK + 1 : BACK + 3]
    back_refs = refs[BACK + 3 : 2 * BACK + 3]
    bias_ref, ratio_ref = refs[2 * BACK + 3 :]

    @pl.when(pl.program_id(0) == 0)
    def _():
        bias_ref[...] = mask_bias(here_ref[0], len_ref[...])
        ratio_ref[...] = jnp.broadcast_to(ratio_column(old_ref, new_ref), (TOKENS, HEAD))

    keys = jnp.concatenate([r[0] for r in kv_refs], axis=0)
    values = jnp.concatenate([r[1] for r in kv_refs], axis=0)
    keys_t = keys.T
    bias = jnp.concatenate([bias_ref[...]] * 2, axis=1)
    ratio = jnp.concatenate([ratio_ref[...]] * 2, axis=0)
    dk = jnp.zeros((SPAN, HEAD), F32)
    dv = jnp.zeros((SPAN, HEAD), F32)
    for pair in range(GROUP // 2):
        q = pair_rows(q_ref, pair)
        grad = (pair_rows(g_ref, pair).astype(F32) * ratio).astype(BF)
        logs = jnp.concatenate([log_ref[0, 2 * pair : 2 * pair + 1, :], log_ref[0, 2 * pair + 1 : 2 * pair + 2, :]], axis=1)
        p = jnp.exp2(scores_of(keys, q, bias) - logs)
        dp = dot_nt(values, grad)
        delta = jnp.sum(p * dp, axis=0, keepdims=True)
        ds = (p * (dp - delta)).astype(BF)
        dv = dv + dot(p.astype(BF), grad)
        dk = dk + dot(ds, q)
        dq_t = dot(keys_t, ds) * SCALE
        for i in range(2):
            h = 2 * pair + i
            dq_ref[:, h * HEAD : (h + 1) * HEAD] = dq_t[:, i * TOKENS : (i + 1) * TOKENS].T
    dk = dk * SCALE
    own_ref[0] = dk[BACK * TOKENS :]
    own_ref[1] = dv[BACK * TOKENS :]
    for j, ref in enumerate(back_refs):
        at = (BACK - 1 - j) * TOKENS
        ref[0] = dk[at : at + TOKENS].astype(BF)
        ref[1] = dv[at : at + TOKENS].astype(BF)


def params(mib):
    return pltpu.CompilerParams(vmem_limit_bytes=mib * 2**20)


KV_SPEC = pl.BlockSpec((2, TOKENS, HEAD), lambda g, *_: (0, 0, g))
ROW_SPEC = pl.BlockSpec((1, TOKENS), lambda g, *_: (0, 0))
Q_SPEC = pl.BlockSpec((TOKENS, GROUP * HEAD), lambda g, *_: (0, g))
LOG_SPEC = pl.BlockSpec((1, GROUP, TOKENS), lambda g, *_: (g, 0, 0))


def attention_forward(here, lengths, q, kvs):
    rows = q.shape[1]
    return pl.pallas_call(
        forward_kernel,
        grid_spec=pltpu.PrefetchScalarGridSpec(
            num_scalar_prefetch=1,
            grid=(KV_HEADS,),
            in_specs=[ROW_SPEC, Q_SPEC] + [KV_SPEC] * (BACK + 1),
            out_specs=[pl.BlockSpec((GROUP * HEAD, TOKENS), lambda g, *_: (g, 0)), LOG_SPEC],
            scratch_shapes=[pltpu.VMEM((SPAN, TOKENS), F32)],
        ),
        out_shape=[
            jax.ShapeDtypeStruct((rows, TOKENS), BF),
            jax.ShapeDtypeStruct((KV_HEADS, GROUP, TOKENS), F32),
        ],
        compiler_params=params(10),
        cost_estimate=pl.CostEstimate(flops=2 * 2 * 32 * 128 * 640 * 128, bytes_accessed=2**22, transcendentals=32 * 128 * 640),
        name="attention_forward",
    )(here, lengths, q, *kvs)


def attention_backward(here, lengths, old, new, q, g, logs, kvs):
    kv_shape = (2, TOKENS, KV_HEADS * HEAD)
    return pl.pallas_call(
        backward_kernel,
        grid_spec=pltpu.PrefetchScalarGridSpec(
            num_scalar_prefetch=1,
            grid=(KV_HEADS,),
            in_specs=[ROW_SPEC, ROW_SPEC, ROW_SPEC, Q_SPEC, Q_SPEC, LOG_SPEC] + [KV_SPEC] * (BACK + 1),
            out_specs=[Q_SPEC, KV_SPEC] + [KV_SPEC] * BACK,
            scratch_shapes=[pltpu.VMEM((SPAN, TOKENS), F32), pltpu.VMEM((TOKENS, HEAD), F32)],
        ),
        out_shape=[
            jax.ShapeDtypeStruct(q.shape, F32),
            jax.ShapeDtypeStruct(kv_shape, F32),
        ]
        + [jax.ShapeDtypeStruct(kv_shape, BF)] * BACK,
        compiler_params=params(14),
        cost_estimate=pl.CostEstimate(flops=5 * 2 * 32 * 128 * 640 * 128, bytes_accessed=2**23, transcendentals=32 * 128 * 640),
        name="attention_backward",
    )(here, lengths, old, new, q, g, logs, *kvs)


def along_tokens(v, by):
    count = math.prod(lax.axis_size(axis) for axis in FLAT)
    return lax.ppermute(v, FLAT, [(i, i + by) for i in range(count) if 0 <= i + by < count])


def moved(v, to):
    sizes = [lax.axis_size(axis) for axis in FLAT]
    pairs = []
    for i, at in enumerate(itertools.product(*map(range, sizes))):
        there = to(*at)
        if there is not None:
            pairs.append((i, sum(c * math.prod(sizes[j + 1 :]) for j, c in enumerate(there))))
    return lax.ppermute(v, FLAT, pairs)


def core_swap(v):
    return moved(v, lambda zh, x, c, zl, y: (zh, x, 1 - c, zl, y))


def group_turn(v, by):
    return moved(v, lambda zh, x, c, zl, y: (zh, (x + by * c) % RING, c, zl, (y + by * (1 - c)) % RING))


def reduce_turn(v, by):
    return moved(v, lambda zh, x, c, zl, y: (zh, (x + by * (1 - c)) % RING, c, zl, (y + by * c) % RING))


def transposed(v):
    return moved(v, lambda zh, x, c, zl, y: (zh, y, c, zl, x) if c == 1 and x != y else None)


def weigh_kernel(core_ref, old_ref, new_ref, cot_ref, keep_ref, send_ref):
    ratio = ratio_column(old_ref, new_ref)
    for out_ref, half in ((keep_ref, core_ref[0]), (send_ref, 1 - core_ref[0])):
        for chunk in range(RING):
            for zh in range(ZH):
                at = pl.multiple_of((zh * 2 * RING + chunk * 2 + half) * HEAD, HEAD)
                to = (chunk * ZH + zh) * HEAD
                part = cot_ref[:, pl.ds(at, HEAD)].astype(F32) * ratio
                out_ref[:, to : to + HEAD] = part.astype(BF)


def weigh(core, old, new, cotangent):
    half = jax.ShapeDtypeStruct((TOKENS, cotangent.shape[1] // 2), BF)
    smem = pl.BlockSpec(memory_space=pltpu.SMEM)
    vmem = pl.BlockSpec(memory_space=pltpu.VMEM)
    return pl.pallas_call(
        weigh_kernel,
        in_specs=[smem, vmem, vmem, vmem],
        out_specs=[vmem, vmem],
        out_shape=[half, half],
        compiler_params=params(8),
        cost_estimate=pl.CostEstimate(flops=2**20, bytes_accessed=2**21, transcendentals=0),
        name="weigh",
    )(core, old, new, cotangent)


def product_kernel(first_ref, *refs):
    o_refs, w_refs, out_refs = refs[:RING], refs[RING : 2 * RING], refs[2 * RING :]
    lhs = jnp.concatenate([r[c].reshape(ROWS, TOKENS) for r in o_refs for c in range(2)], axis=1)
    rhs = jnp.concatenate([r[...] for r in w_refs], axis=0)
    part = dot(lhs, rhs).astype(BF)
    for step, ref in enumerate(out_refs):

        @pl.when(pl.program_id(0) == step)
        def _(ref=ref):
            for zh in range(ZH):
                for zl in range(ZL):
                    ref[zh * ZL + zl] = part[zl * ROWS // ZL : (zl + 1) * ROWS // ZL, zh * HEAD : (zh + 1) * HEAD]


def product(first, count, outs, ws):
    chunk = (ZH * ZL, ROWS // ZL, HEAD)
    width = ZH * HEAD
    return pl.pallas_call(
        product_kernel,
        grid_spec=pltpu.PrefetchScalarGridSpec(
            num_scalar_prefetch=1,
            grid=(count,),
            in_specs=[pl.BlockSpec((2, ZL, ROWS // ZL, TOKENS), lambda i, f: (0, 0, 0, 0), pipeline_mode=pl.Buffered(1))] * RING
            + [pl.BlockSpec((2 * TOKENS, width), lambda i, f: (0, lax.rem(f[0] + i, RING)))] * RING,
            out_specs=[pl.BlockSpec(chunk, lambda i, f: (0, 0, 0), pipeline_mode=pl.Buffered(1))] * count,
        ),
        out_shape=[jax.ShapeDtypeStruct(chunk, BF)] * count,
        compiler_params=params(22),
        cost_estimate=pl.CostEstimate(flops=2 * ROWS * 1024 * width * count, bytes_accessed=2**21 * (1 + count), transcendentals=0),
        name="product",
    )(first, *outs, *ws)


def shards(queries, keys, values, head_grads, cotangent, old, new, doc_lengths):
    here = lax.axis_index(FLAT).astype(jnp.int32).reshape(1)
    lengths = doc_lengths.reshape(1, -1)
    old = old.reshape(1, -1)
    new = new.reshape(1, -1)
    core, x, y = (lax.axis_index(a).astype(jnp.int32) for a in ("core", "x", "y"))
    in_group = jnp.where(core == 0, y, x)
    in_reduce = jnp.where(core == 0, x, y)

    kv = jnp.stack([keys, values])
    kvs = [along_tokens(kv, by) for by in range(BACK, 0, -1)] + [kv]

    kv, cotangent = lax.optimization_barrier((kv, cotangent))
    keep, send = weigh(core.reshape(1), old, new, cotangent)
    w_mine = jnp.concatenate([keep, core_swap(send)], axis=0)
    ws = [w_mine] + [group_turn(w_mine, by) for by in range(1, RING)]

    here_after, ws[2] = lax.optimization_barrier((here, ws[2]))
    out_t, logs = attention_forward(here_after, lengths, queries, kvs)
    out_both = jnp.stack([out_t, core_swap(out_t)]).reshape(2, ZL, RING, ROWS // ZL, TOKENS)

    def rows_of(by):
        return lax.dynamic_index_in_dim(out_both, (in_group + by) % RING, 2, keepdims=False)

    outs = [rows_of(0)] + [group_turn(rows_of(by), by) for by in range(1, RING)]

    dq, own, *backs = attention_backward(here, lengths, old, new, queries, head_grads, logs, kvs)
    *outs, own = lax.optimization_barrier((*outs, own))
    home = [along_tokens(b, -(j + 1)) for j, b in enumerate(backs)]

    sent = product(((in_reduce + 1) % RING).reshape(1), RING - 1, outs, ws)
    got = [reduce_turn(part, by) for by, part in enumerate(sent, 1)]
    (mine,) = product(in_reduce.reshape(1), 1, outs, ws)
    part = sum((g.astype(F32) for g in got), mine.astype(F32)).astype(BF)
    *home, part = lax.optimization_barrier((*home, part))
    part = lax.all_to_all(part, ("zh", "zl"), split_axis=0, concat_axis=0, tiled=True)
    total = jnp.sum(part.astype(F32), axis=0).astype(BF)

    dkv = own + sum(b.astype(F32) for b in home)
    grad_weight = jnp.where((core == 1) & (x != y), transposed(total), total).astype(F32)
    return dq, dkv[0], dkv[1], grad_weight


def solution(mesh):
    mesh = Mesh(mesh.devices.reshape(ZH, RING, 2, ZL, RING), FLAT)
    tokens = P(FLAT, None)
    return jax.shard_map(
        shards,
        mesh=mesh,
        in_specs=(tokens, tokens, tokens, tokens, tokens, P(FLAT), P(FLAT), P()),
        out_specs=(tokens, tokens, tokens, P(("zl", "y"), ("zh", "x", "core"))),
        check_vma=False,
    )
```

```python
import itertools
import math

import jax
import jax.numpy as jnp
from jax import lax
from jax.experimental import pallas as pl
from jax.experimental.pallas import tpu as pltpu
from jax.sharding import Mesh, PartitionSpec as P

HEAD = 128
TOKENS = 128
BACK = 4
SPAN = (BACK + 1) * TOKENS
KV_HEADS = 4
GROUP = 8
ZH, ZL, RING = 4, 2, 4
ROWS = 1024
FORWARD_MIB, BACKWARD_MIB, PREPARE_MIB, PRODUCT_MIB = 56, 56, 56, 56
AFTER = 3
CLIP = 2.0
NEG = -1e30
SCALE = 1.0 / math.sqrt(HEAD)
LOG2E = math.log2(math.e)
FLAT = ("zh", "x", "core", "zl", "y")
BF = jnp.bfloat16
F32 = jnp.float32

NT = (((1,), (1,)), ((), ()))


def dot(a, b):
    return jnp.dot(a, b, preferred_element_type=F32)


def dot_nt(a, b):
    return lax.dot_general(a, b, NT, preferred_element_type=F32)


def mask_bias(here, lengths):
    row = lax.broadcasted_iota(jnp.int32, (TOKENS, TOKENS), 0)
    col = lax.broadcasted_iota(jnp.int32, (TOKENS, TOKENS), 1)
    lens = jnp.broadcast_to(lengths.astype(F32), (TOKENS, TOKENS))
    ends = jnp.sum(jnp.where(col <= row, lens, 0.0), axis=1, keepdims=True)
    lens_col = jnp.sum(jnp.where(col == row, lens, 0.0), axis=1, keepdims=True)
    base = here * TOKENS
    pos = (base + col).astype(F32)
    first = jnp.sum(jnp.where(ends <= pos, lens_col, 0.0), axis=0, keepdims=True)
    first = first.astype(jnp.int32)
    key = base - BACK * TOKENS + lax.broadcasted_iota(jnp.int32, (SPAN, TOKENS), 0)
    query = base + lax.broadcasted_iota(jnp.int32, (SPAN, TOKENS), 1)
    seen = (key <= query) & (key >= first)
    return jnp.where(seen, 0.0, NEG)


def scores_of(keys, q_pair, bias):
    return dot_nt(keys, q_pair) * (SCALE * LOG2E) + bias


def pair_rows(ref_or_val, pair):
    a = ref_or_val[:, (2 * pair) * HEAD : (2 * pair + 1) * HEAD]
    b = ref_or_val[:, (2 * pair + 1) * HEAD : (2 * pair + 2) * HEAD]
    return jnp.concatenate([a, b], axis=0)


def forward_kernel(here_ref, len_ref, q_ref, *refs):
    kv_refs = refs[: BACK + 1]
    own_refs = refs[BACK + 1 : BACK + 1 + RING]
    cross_refs = refs[BACK + 1 + RING : BACK + 1 + 2 * RING]
    log_ref, bias_ref = refs[BACK + 1 + 2 * RING :]
    g = pl.program_id(0)

    @pl.when(g == 0)
    def _():
        bias_ref[...] = mask_bias(here_ref[0], len_ref[...])

    keys = jnp.concatenate([r[0] for r in kv_refs], axis=0)
    values_t = jnp.concatenate([r[1] for r in kv_refs], axis=0).T
    bias = jnp.concatenate([bias_ref[...]] * 2, axis=1)
    zl = g // 2
    quads = []
    for pair in range(GROUP // 2):
        s = scores_of(keys, pair_rows(q_ref, pair), bias)
        top = jnp.max(s, axis=0, keepdims=True)
        p = jnp.exp2(s - top)
        total = jnp.sum(p, axis=0, keepdims=True)
        out_t = (dot(values_t, p.astype(BF)) / total).astype(BF)
        log_total = top + jnp.log2(total)
        for i in range(2):
            h = 2 * pair + i
            quads.append(out_t[:, i * TOKENS : (i + 1) * TOKENS])
            log_ref[0, h : h + 1, :] = log_total[:, i * TOKENS : (i + 1) * TOKENS]
    for u in range(2):
        quad = jnp.concatenate(quads[4 * u : 4 * u + 4], axis=0)
        row_group = lax.rem(2 * g + u, RING)
        for group, out_refs in ((here_ref[1], own_refs), (here_ref[2], cross_refs)):
            away = lax.rem(row_group - group + RING, RING)
            for k, ref in enumerate(out_refs):

                @pl.when(away == k)
                def _(ref=ref, quad=quad):
                    ref[zl] = quad


def column_of(row):
    r = lax.broadcasted_iota(jnp.int32, (TOKENS, TOKENS), 0)
    c = lax.broadcasted_iota(jnp.int32, (TOKENS, TOKENS), 1)
    return jnp.sum(jnp.where(r == c, jnp.broadcast_to(row, (TOKENS, TOKENS)), 0.0), axis=1, keepdims=True)


def ratio_column(old_ref, new_ref):
    return column_of(jnp.minimum(jnp.exp(new_ref[...] - old_ref[...]), CLIP))


def backward_kernel(here_ref, len_ref, old_ref, new_ref, q_ref, g_ref, log_ref, *refs):
    kv_refs = refs[: BACK + 1]
    dq_ref, own_ref = refs[BACK + 1 : BACK + 3]
    back_refs = refs[BACK + 3 : 2 * BACK + 3]
    bias_ref, ratio_ref = refs[2 * BACK + 3 :]

    @pl.when(pl.program_id(0) == 0)
    def _():
        bias_ref[...] = mask_bias(here_ref[0], len_ref[...])
        ratio_ref[...] = jnp.broadcast_to(ratio_column(old_ref, new_ref), (TOKENS, HEAD))

    keys = jnp.concatenate([r[0] for r in kv_refs], axis=0)
    values = jnp.concatenate([r[1] for r in kv_refs], axis=0)
    keys_t = keys.T
    bias = jnp.concatenate([bias_ref[...]] * 2, axis=1)
    ratio = jnp.concatenate([ratio_ref[...]] * 2, axis=0)
    dk = jnp.zeros((SPAN, HEAD), F32)
    dv = jnp.zeros((SPAN, HEAD), F32)
    for pair in range(GROUP // 2):
        q = pair_rows(q_ref, pair)
        grad = (pair_rows(g_ref, pair).astype(F32) * ratio).astype(BF)
        logs = jnp.concatenate([log_ref[0, 2 * pair : 2 * pair + 1, :], log_ref[0, 2 * pair + 1 : 2 * pair + 2, :]], axis=1)
        p = jnp.exp2(scores_of(keys, q, bias) - logs)
        dp = dot_nt(values, grad)
        delta = jnp.sum(p * dp, axis=0, keepdims=True)
        ds = (p * (dp - delta)).astype(BF)
        dv = dv + dot(p.astype(BF), grad)
        dk = dk + dot(ds, q)
        dq_t = dot(keys_t, ds) * SCALE
        for i in range(2):
            h = 2 * pair + i
            dq_ref[:, h * HEAD : (h + 1) * HEAD] = dq_t[:, i * TOKENS : (i + 1) * TOKENS].T
    dk = dk * SCALE
    own_ref[0] = dk[BACK * TOKENS :]
    own_ref[1] = dv[BACK * TOKENS :]
    for j, ref in enumerate(back_refs):
        at = (BACK - 1 - j) * TOKENS
        ref[0] = dk[at : at + TOKENS].astype(BF)
        ref[1] = dv[at : at + TOKENS].astype(BF)


def params(mib):
    return pltpu.CompilerParams(vmem_limit_bytes=mib * 2**20)


KV_SPEC = pl.BlockSpec((2, TOKENS, HEAD), lambda g, *_: (0, 0, g))
ROW_SPEC = pl.BlockSpec((1, TOKENS), lambda g, *_: (0, 0))
Q_SPEC = pl.BlockSpec((TOKENS, GROUP * HEAD), lambda g, *_: (0, g))
LOG_SPEC = pl.BlockSpec((1, GROUP, TOKENS), lambda g, *_: (g, 0, 0))


def attention_forward(place, lengths, q, kvs):
    piece = (ZL, ROWS // ZL, TOKENS)
    out = pl.pallas_call(
        forward_kernel,
        grid_spec=pltpu.PrefetchScalarGridSpec(
            num_scalar_prefetch=1,
            grid=(KV_HEADS,),
            in_specs=[ROW_SPEC, Q_SPEC] + [KV_SPEC] * (BACK + 1),
            out_specs=[pl.BlockSpec(piece, lambda g, *_: (0, 0, 0))] * (2 * RING) + [LOG_SPEC],
            scratch_shapes=[pltpu.VMEM((SPAN, TOKENS), F32)],
        ),
        out_shape=[jax.ShapeDtypeStruct(piece, BF)] * (2 * RING)
        + [jax.ShapeDtypeStruct((KV_HEADS, GROUP, TOKENS), F32)],
        compiler_params=params(FORWARD_MIB),
        cost_estimate=pl.CostEstimate(flops=2 * 2 * 32 * 128 * 640 * 128, bytes_accessed=2**22, transcendentals=32 * 128 * 640),
        name="attention_forward",
    )(place, lengths, q, *kvs)
    return out[:RING], out[RING : 2 * RING], out[2 * RING]


def attention_backward(here, lengths, old, new, q, g, logs, kvs):
    kv_shape = (2, TOKENS, KV_HEADS * HEAD)
    return pl.pallas_call(
        backward_kernel,
        grid_spec=pltpu.PrefetchScalarGridSpec(
            num_scalar_prefetch=1,
            grid=(KV_HEADS,),
            in_specs=[ROW_SPEC, ROW_SPEC, ROW_SPEC, Q_SPEC, Q_SPEC, LOG_SPEC] + [KV_SPEC] * (BACK + 1),
            out_specs=[Q_SPEC, KV_SPEC] + [KV_SPEC] * BACK,
            scratch_shapes=[pltpu.VMEM((SPAN, TOKENS), F32), pltpu.VMEM((TOKENS, HEAD), F32)],
        ),
        out_shape=[
            jax.ShapeDtypeStruct(q.shape, F32),
            jax.ShapeDtypeStruct(kv_shape, F32),
        ]
        + [jax.ShapeDtypeStruct(kv_shape, BF)] * BACK,
        compiler_params=params(BACKWARD_MIB),
        cost_estimate=pl.CostEstimate(flops=5 * 2 * 32 * 128 * 640 * 128, bytes_accessed=2**23, transcendentals=32 * 128 * 640),
        name="attention_backward",
    )(here, lengths, old, new, q, g, logs, *kvs)


def along_tokens(v, by):
    count = math.prod(lax.axis_size(axis) for axis in FLAT)
    return lax.ppermute(v, FLAT, [(i, i + by) for i in range(count) if 0 <= i + by < count])


def moved(v, to):
    sizes = [lax.axis_size(axis) for axis in FLAT]
    pairs = []
    for i, at in enumerate(itertools.product(*map(range, sizes))):
        there = to(*at)
        if there is not None:
            pairs.append((i, sum(c * math.prod(sizes[j + 1 :]) for j, c in enumerate(there))))
    return lax.ppermute(v, FLAT, pairs)


def core_swap(v):
    return moved(v, lambda zh, x, c, zl, y: (zh, x, 1 - c, zl, y))


def group_turn(v, by):
    return moved(v, lambda zh, x, c, zl, y: (zh, (x + by * c) % RING, c, zl, (y + by * (1 - c)) % RING))


def cross_turn(v, by):
    return moved(v, lambda zh, x, c, zl, y: (zh, (x + by * (1 - c)) % RING, 1 - c, zl, (y + by * c) % RING))


def reduce_turn(v, by):
    return moved(v, lambda zh, x, c, zl, y: (zh, (x + by * (1 - c)) % RING, c, zl, (y + by * c) % RING))


def transposed(v):
    return moved(v, lambda zh, x, c, zl, y: (zh, y, c, zl, x) if c == 1 and x != y else None)


def brought_home(own, backs, y):
    before = backs[RING - 1].astype(F32)
    for by in range(1, RING):
        part = moved(backs[by - 1], lambda zh, x, c, zl, y: (zh, x, c, zl, (y - by) % RING)).astype(F32)
        here = y + by < RING
        own = own + jnp.where(here, part, 0.0)
        before = before + jnp.where(here, 0.0, part)
    return own + along_tokens(before.astype(BF), -RING).astype(F32)


def prepare_kernel(place_ref, old_ref, new_ref, keys_ref, values_ref, cot_ref, kv_ref, keep_ref, send_ref):
    kv_ref[0] = keys_ref[...]
    kv_ref[1] = values_ref[...]
    ratio = ratio_column(old_ref, new_ref)
    core = place_ref[3]
    for out_ref, half in ((keep_ref, core), (send_ref, 1 - core)):
        for chunk in range(RING):
            for zh in range(ZH):
                at = pl.multiple_of((zh * 2 * RING + chunk * 2 + half) * HEAD, HEAD)
                to = (chunk * ZH + zh) * HEAD
                part = cot_ref[:, pl.ds(at, HEAD)].astype(F32) * ratio
                out_ref[:, to : to + HEAD] = part.astype(BF)


def prepare(place, old, new, keys, values, cotangent):
    half = jax.ShapeDtypeStruct((TOKENS, cotangent.shape[1] // 2), BF)
    smem = pl.BlockSpec(memory_space=pltpu.SMEM)
    vmem = pl.BlockSpec(memory_space=pltpu.VMEM)
    return pl.pallas_call(
        prepare_kernel,
        in_specs=[smem] + [vmem] * 5,
        out_specs=[vmem] * 3,
        out_shape=[jax.ShapeDtypeStruct((2,) + keys.shape, BF), half, half],
        compiler_params=params(PREPARE_MIB),
        cost_estimate=pl.CostEstimate(flops=2**20, bytes_accessed=2**22, transcendentals=0),
        name="prepare",
    )(place, old, new, keys, values, cotangent)


def product_kernel(first_ref, *refs):
    o_refs, w_refs, out_refs = refs[: 2 * RING], refs[2 * RING : 3 * RING], refs[3 * RING :]
    rows = o_refs[0].shape[1]
    lhs = jnp.concatenate([r[...].reshape(ZL * rows, TOKENS) for r in o_refs], axis=1)
    rhs = jnp.concatenate([r[...] for r in w_refs], axis=0)
    part = dot(lhs, rhs).astype(BF)
    for step, ref in enumerate(out_refs):

        @pl.when(pl.program_id(0) == step)
        def _(ref=ref):
            for zh in range(ZH):
                for zl in range(ZL):
                    ref[zh * ZL + zl] = part[zl * rows : (zl + 1) * rows, zh * HEAD : (zh + 1) * HEAD]


def product(first, count, outs, ws):
    rows = ROWS // ZL
    chunk = (ZH * ZL, rows, HEAD)
    width = ZH * HEAD
    return pl.pallas_call(
        product_kernel,
        grid_spec=pltpu.PrefetchScalarGridSpec(
            num_scalar_prefetch=1,
            grid=(count,),
            in_specs=[pl.BlockSpec((ZL, rows, TOKENS), lambda i, f: (0, 0, 0), pipeline_mode=pl.Buffered(1))] * (2 * RING)
            + [pl.BlockSpec((2 * TOKENS, width), lambda i, f: (0, lax.rem(f[0] + i, RING)))] * RING,
            out_specs=[pl.BlockSpec(chunk, lambda i, f: (0, 0, 0), pipeline_mode=pl.Buffered(1))] * count,
        ),
        out_shape=[jax.ShapeDtypeStruct(chunk, BF)] * count,
        compiler_params=params(PRODUCT_MIB),
        cost_estimate=pl.CostEstimate(flops=2 * ZL * rows * 1024 * width * count, bytes_accessed=2**21 * (1 + count), transcendentals=0),
        name="product",
    )(first, *outs, *ws)


def shards(queries, keys, values, head_grads, cotangent, old, new, doc_lengths):
    here = lax.axis_index(FLAT).astype(jnp.int32)
    lengths = doc_lengths.reshape(1, -1)
    old = old.reshape(1, -1)
    new = new.reshape(1, -1)
    core, x, y = (lax.axis_index(a).astype(jnp.int32) for a in ("core", "x", "y"))
    in_group = jnp.where(core == 0, y, x)
    in_reduce = jnp.where(core == 0, x, y)
    place = jnp.stack([here, in_group, in_reduce, core])

    kv, keep, send = prepare(place, old, new, keys, values, cotangent)
    kvs = [along_tokens(kv, by) for by in range(BACK, 0, -1)] + [kv]
    w_mine = jnp.concatenate([keep, core_swap(send)], axis=0)
    kvs[AFTER], w_soon = lax.optimization_barrier((kvs[AFTER], w_mine))
    *kvs, w_late = lax.optimization_barrier((*kvs, w_mine))
    ws = [w_mine] + [group_turn(w_soon if by == 2 else w_late, by) for by in range(1, RING)]

    same, cross, logs = attention_forward(place, lengths, queries, kvs)
    dq, own, *backs = attention_backward(place, lengths, old, new, queries, head_grads, logs, kvs)
    *pieces, ws[1], ws[2], ws[3], own = lax.optimization_barrier((*same, *cross, *ws[1:], own))
    same, cross = pieces[:RING], pieces[RING:]
    outs = []
    for by in range(RING):
        outs.append(group_turn(same[by], by) if by else same[0])
        outs.append(cross_turn(cross[by], by))

    first = ((in_reduce + 1) % RING).reshape(1)
    sent = product(first, RING - 1, outs, ws)
    got = [reduce_turn(part, by) for by, part in enumerate(sent, 1)]

    (mine,) = product(in_reduce.reshape(1), 1, outs, ws)
    part = sum((g.astype(F32) for g in got), mine.astype(F32)).astype(BF)
    dkv = brought_home(own, backs, y)
    dkv, part = lax.optimization_barrier((dkv, part))
    part = lax.all_to_all(part, ("zh", "zl"), split_axis=0, concat_axis=0, tiled=True)
    total = jnp.sum(part.astype(F32), axis=0).astype(BF)

    grad_weight = jnp.where((core == 1) & (x != y), transposed(total), total).astype(F32)
    return dq, dkv[0], dkv[1], grad_weight


def solution(mesh):
    mesh = Mesh(mesh.devices.reshape(ZH, RING, 2, ZL, RING), FLAT)
    tokens = P(FLAT, None)
    return jax.shard_map(
        shards,
        mesh=mesh,
        in_specs=(tokens, tokens, tokens, tokens, tokens, P(FLAT), P(FLAT), P()),
        out_specs=(tokens, tokens, tokens, P(("zl", "y"), ("zh", "x", "core"))),
        check_vma=False,
    )
```

```python
import itertools
import math

import jax
import jax.numpy as jnp
from jax import lax
from jax.experimental import pallas as pl
from jax.experimental.pallas import tpu as pltpu
from jax.sharding import Mesh, PartitionSpec as P

HEAD = 128
TOKENS = 128
BACK = 4
SPAN = (BACK + 1) * TOKENS
KV_HEADS = 4
GROUP = 8
HEADS_AT_ONCE = 8
ZH, ZL, RING = 4, 2, 4
ROWS = 1024
FORWARD_MIB, BACKWARD_MIB, PREPARE_MIB, PRODUCT_MIB = 56, 56, 56, 56
AFTER = 3
CLIP = 2.0
NEG = -1e30
SCALE = 1.0 / math.sqrt(HEAD)
LOG2E = math.log2(math.e)
FLAT = ("zh", "x", "core", "zl", "y")
BF = jnp.bfloat16
F32 = jnp.float32

NT = (((1,), (1,)), ((), ()))


def dot(a, b):
    return jnp.dot(a, b, preferred_element_type=F32)


def dot_nt(a, b):
    return lax.dot_general(a, b, NT, preferred_element_type=F32)


def mask_bias(here, lengths):
    row = lax.broadcasted_iota(jnp.int32, (TOKENS, TOKENS), 0)
    col = lax.broadcasted_iota(jnp.int32, (TOKENS, TOKENS), 1)
    lens = jnp.broadcast_to(lengths.astype(F32), (TOKENS, TOKENS))
    ends = jnp.sum(jnp.where(col <= row, lens, 0.0), axis=1, keepdims=True)
    lens_col = jnp.sum(jnp.where(col == row, lens, 0.0), axis=1, keepdims=True)
    base = here * TOKENS
    pos = (base + col).astype(F32)
    first = jnp.sum(jnp.where(ends <= pos, lens_col, 0.0), axis=0, keepdims=True)
    first = first.astype(jnp.int32)
    key = base - BACK * TOKENS + lax.broadcasted_iota(jnp.int32, (SPAN, TOKENS), 0)
    query = base + lax.broadcasted_iota(jnp.int32, (SPAN, TOKENS), 1)
    seen = (key <= query) & (key >= first)
    return jnp.where(seen, 0.0, NEG)


def scores_of(keys, q_pair, bias):
    return dot_nt(keys, q_pair) * (SCALE * LOG2E) + bias


def rows_of_heads(ref, at, count):
    return jnp.concatenate([ref[:, h * HEAD : (h + 1) * HEAD] for h in range(at, at + count)], axis=0)


def forward_kernel(here_ref, len_ref, q_ref, *refs):
    kv_refs = refs[: BACK + 1]
    own_refs = refs[BACK + 1 : BACK + 1 + RING]
    cross_refs = refs[BACK + 1 + RING : BACK + 1 + 2 * RING]
    log_ref, bias_ref = refs[BACK + 1 + 2 * RING :]
    g = pl.program_id(0)

    @pl.when(g == 0)
    def _():
        bias_ref[...] = mask_bias(here_ref[0], len_ref[...])

    keys = jnp.concatenate([r[0] for r in kv_refs], axis=0)
    values_t = jnp.concatenate([r[1] for r in kv_refs], axis=0).T
    bias = jnp.concatenate([bias_ref[...]] * HEADS_AT_ONCE, axis=1)
    zl = g // 2
    quads = []
    for at in range(0, GROUP, HEADS_AT_ONCE):
        s = scores_of(keys, rows_of_heads(q_ref, at, HEADS_AT_ONCE), bias)
        top = jnp.max(s, axis=0, keepdims=True)
        p = jnp.exp2(s - top)
        total = jnp.sum(p, axis=0, keepdims=True)
        out_t = (dot(values_t, p.astype(BF)) / total).astype(BF)
        log_total = top + jnp.log2(total)
        for i in range(HEADS_AT_ONCE):
            h = at + i
            quads.append(out_t[:, i * TOKENS : (i + 1) * TOKENS])
            log_ref[0, h : h + 1, :] = log_total[:, i * TOKENS : (i + 1) * TOKENS]
    for u in range(2):
        quad = jnp.concatenate(quads[4 * u : 4 * u + 4], axis=0)
        row_group = lax.rem(2 * g + u, RING)
        for group, out_refs in ((here_ref[1], own_refs), (here_ref[2], cross_refs)):
            away = lax.rem(row_group - group + RING, RING)
            for k, ref in enumerate(out_refs):

                @pl.when(away == k)
                def _(ref=ref, quad=quad):
                    ref[zl] = quad


def column_of(row):
    r = lax.broadcasted_iota(jnp.int32, (TOKENS, TOKENS), 0)
    c = lax.broadcasted_iota(jnp.int32, (TOKENS, TOKENS), 1)
    return jnp.sum(jnp.where(r == c, jnp.broadcast_to(row, (TOKENS, TOKENS)), 0.0), axis=1, keepdims=True)


def ratio_column(old_ref, new_ref):
    return column_of(jnp.minimum(jnp.exp(new_ref[...] - old_ref[...]), CLIP))


def backward_kernel(here_ref, len_ref, old_ref, new_ref, q_ref, g_ref, log_ref, *refs):
    kv_refs = refs[: BACK + 1]
    dq_ref, own_ref = refs[BACK + 1 : BACK + 3]
    back_refs = refs[BACK + 3 : 2 * BACK + 3]
    bias_ref, ratio_ref = refs[2 * BACK + 3 :]

    @pl.when(pl.program_id(0) == 0)
    def _():
        bias_ref[...] = mask_bias(here_ref[0], len_ref[...])
        ratio_ref[...] = jnp.broadcast_to(ratio_column(old_ref, new_ref), (TOKENS, HEAD))

    keys = jnp.concatenate([r[0] for r in kv_refs], axis=0)
    values = jnp.concatenate([r[1] for r in kv_refs], axis=0)
    keys_t = keys.T
    bias = jnp.concatenate([bias_ref[...]] * HEADS_AT_ONCE, axis=1)
    ratio = jnp.concatenate([ratio_ref[...]] * HEADS_AT_ONCE, axis=0)
    dk = jnp.zeros((SPAN, HEAD), F32)
    dv = jnp.zeros((SPAN, HEAD), F32)
    for at in range(0, GROUP, HEADS_AT_ONCE):
        q = rows_of_heads(q_ref, at, HEADS_AT_ONCE)
        grad = (rows_of_heads(g_ref, at, HEADS_AT_ONCE).astype(F32) * ratio).astype(BF)
        logs = jnp.concatenate([log_ref[0, h : h + 1, :] for h in range(at, at + HEADS_AT_ONCE)], axis=1)
        p = jnp.exp2(scores_of(keys, q, bias) - logs)
        dp = dot_nt(values, grad)
        delta = jnp.sum(p * dp, axis=0, keepdims=True)
        ds = (p * (dp - delta)).astype(BF)
        dv = dv + dot(p.astype(BF), grad)
        dk = dk + dot(ds, q)
        dq_t = dot(keys_t, ds) * SCALE
        for i in range(HEADS_AT_ONCE):
            h = at + i
            dq_ref[:, h * HEAD : (h + 1) * HEAD] = dq_t[:, i * TOKENS : (i + 1) * TOKENS].T
    dk = dk * SCALE
    own_ref[0] = dk[BACK * TOKENS :]
    own_ref[1] = dv[BACK * TOKENS :]
    for j, ref in enumerate(back_refs):
        at = (BACK - 1 - j) * TOKENS
        ref[0] = dk[at : at + TOKENS].astype(BF)
        ref[1] = dv[at : at + TOKENS].astype(BF)


def params(mib):
    return pltpu.CompilerParams(vmem_limit_bytes=mib * 2**20)


KV_SPEC = pl.BlockSpec((2, TOKENS, HEAD), lambda g, *_: (0, 0, g))
ROW_SPEC = pl.BlockSpec((1, TOKENS), lambda g, *_: (0, 0))
Q_SPEC = pl.BlockSpec((TOKENS, GROUP * HEAD), lambda g, *_: (0, g))
LOG_SPEC = pl.BlockSpec((1, GROUP, TOKENS), lambda g, *_: (g, 0, 0))


def attention_forward(place, lengths, q, kvs):
    piece = (ZL, ROWS // ZL, TOKENS)
    out = pl.pallas_call(
        forward_kernel,
        grid_spec=pltpu.PrefetchScalarGridSpec(
            num_scalar_prefetch=1,
            grid=(KV_HEADS,),
            in_specs=[ROW_SPEC, Q_SPEC] + [KV_SPEC] * (BACK + 1),
            out_specs=[pl.BlockSpec(piece, lambda g, *_: (0, 0, 0))] * (2 * RING) + [LOG_SPEC],
            scratch_shapes=[pltpu.VMEM((SPAN, TOKENS), F32)],
        ),
        out_shape=[jax.ShapeDtypeStruct(piece, BF)] * (2 * RING)
        + [jax.ShapeDtypeStruct((KV_HEADS, GROUP, TOKENS), F32)],
        compiler_params=params(FORWARD_MIB),
        cost_estimate=pl.CostEstimate(flops=2 * 2 * 32 * 128 * 640 * 128, bytes_accessed=2**22, transcendentals=32 * 128 * 640),
        name="attention_forward",
    )(place, lengths, q, *kvs)
    return out[:RING], out[RING : 2 * RING], out[2 * RING]


def attention_backward(here, lengths, old, new, q, g, logs, kvs):
    kv_shape = (2, TOKENS, KV_HEADS * HEAD)
    return pl.pallas_call(
        backward_kernel,
        grid_spec=pltpu.PrefetchScalarGridSpec(
            num_scalar_prefetch=1,
            grid=(KV_HEADS,),
            in_specs=[ROW_SPEC, ROW_SPEC, ROW_SPEC, Q_SPEC, Q_SPEC, LOG_SPEC] + [KV_SPEC] * (BACK + 1),
            out_specs=[Q_SPEC, KV_SPEC] + [KV_SPEC] * BACK,
            scratch_shapes=[pltpu.VMEM((SPAN, TOKENS), F32), pltpu.VMEM((TOKENS, HEAD), F32)],
        ),
        out_shape=[
            jax.ShapeDtypeStruct(q.shape, F32),
            jax.ShapeDtypeStruct(kv_shape, F32),
        ]
        + [jax.ShapeDtypeStruct(kv_shape, BF)] * BACK,
        compiler_params=params(BACKWARD_MIB),
        cost_estimate=pl.CostEstimate(flops=5 * 2 * 32 * 128 * 640 * 128, bytes_accessed=2**23, transcendentals=32 * 128 * 640),
        name="attention_backward",
    )(here, lengths, old, new, q, g, logs, *kvs)


def along_tokens(v, by):
    count = math.prod(lax.axis_size(axis) for axis in FLAT)
    return lax.ppermute(v, FLAT, [(i, i + by) for i in range(count) if 0 <= i + by < count])


def moved(v, to):
    sizes = [lax.axis_size(axis) for axis in FLAT]
    pairs = []
    for i, at in enumerate(itertools.product(*map(range, sizes))):
        there = to(*at)
        if there is not None:
            pairs.append((i, sum(c * math.prod(sizes[j + 1 :]) for j, c in enumerate(there))))
    return lax.ppermute(v, FLAT, pairs)


def core_swap(v):
    return moved(v, lambda zh, x, c, zl, y: (zh, x, 1 - c, zl, y))


def group_turn(v, by):
    return moved(v, lambda zh, x, c, zl, y: (zh, (x + by * c) % RING, c, zl, (y + by * (1 - c)) % RING))


def cross_turn(v, by):
    return moved(v, lambda zh, x, c, zl, y: (zh, (x + by * (1 - c)) % RING, 1 - c, zl, (y + by * c) % RING))


def reduce_turn(v, by):
    return moved(v, lambda zh, x, c, zl, y: (zh, (x + by * (1 - c)) % RING, c, zl, (y + by * c) % RING))


def transposed(v):
    return moved(v, lambda zh, x, c, zl, y: (zh, y, c, zl, x) if c == 1 and x != y else None)


def y_turn(v, by):
    return moved(v, lambda zh, x, c, zl, y: (zh, x, c, zl, (y + by) % RING))


def from_predecessors(kv, y):
    before = along_tokens(kv, BACK)
    return [before] + [y_turn(jnp.where(y + by < RING, kv, before), by) for by in range(BACK - 1, 0, -1)]


def brought_home(own, backs, y):
    before = backs[RING - 1].astype(F32)
    for by in range(1, RING):
        part = moved(backs[by - 1], lambda zh, x, c, zl, y: (zh, x, c, zl, (y - by) % RING)).astype(F32)
        here = y + by < RING
        own = own + jnp.where(here, part, 0.0)
        before = before + jnp.where(here, 0.0, part)
    return own + along_tokens(before.astype(BF), -RING).astype(F32)


def prepare_kernel(place_ref, old_ref, new_ref, keys_ref, values_ref, cot_ref, kv_ref, keep_ref, send_ref):
    kv_ref[0] = keys_ref[...]
    kv_ref[1] = values_ref[...]
    ratio = ratio_column(old_ref, new_ref)
    core = place_ref[3]
    for out_ref, half in ((keep_ref, core), (send_ref, 1 - core)):
        for chunk in range(RING):
            for zh in range(ZH):
                at = pl.multiple_of((zh * 2 * RING + chunk * 2 + half) * HEAD, HEAD)
                to = (chunk * ZH + zh) * HEAD
                part = cot_ref[:, pl.ds(at, HEAD)].astype(F32) * ratio
                out_ref[:, to : to + HEAD] = part.astype(BF)


def prepare(place, old, new, keys, values, cotangent):
    half = jax.ShapeDtypeStruct((TOKENS, cotangent.shape[1] // 2), BF)
    smem = pl.BlockSpec(memory_space=pltpu.SMEM)
    vmem = pl.BlockSpec(memory_space=pltpu.VMEM)
    return pl.pallas_call(
        prepare_kernel,
        in_specs=[smem] + [vmem] * 5,
        out_specs=[vmem] * 3,
        out_shape=[jax.ShapeDtypeStruct((2,) + keys.shape, BF), half, half],
        compiler_params=params(PREPARE_MIB),
        cost_estimate=pl.CostEstimate(flops=2**20, bytes_accessed=2**22, transcendentals=0),
        name="prepare",
    )(place, old, new, keys, values, cotangent)


def product_kernel(first_ref, *refs):
    o_refs, w_refs, out_refs = refs[: 2 * RING], refs[2 * RING : 3 * RING], refs[3 * RING :]
    rows = o_refs[0].shape[1]
    lhs = jnp.concatenate([r[...].reshape(ZL * rows, TOKENS) for r in o_refs], axis=1)
    rhs = jnp.concatenate([r[...] for r in w_refs], axis=0)
    part = dot(lhs, rhs).astype(BF)
    for step, ref in enumerate(out_refs):

        @pl.when(pl.program_id(0) == step)
        def _(ref=ref):
            for zh in range(ZH):
                for zl in range(ZL):
                    ref[zh * ZL + zl] = part[zl * rows : (zl + 1) * rows, zh * HEAD : (zh + 1) * HEAD]


def product(first, count, outs, ws):
    rows = ROWS // ZL
    chunk = (ZH * ZL, rows, HEAD)
    width = ZH * HEAD
    return pl.pallas_call(
        product_kernel,
        grid_spec=pltpu.PrefetchScalarGridSpec(
            num_scalar_prefetch=1,
            grid=(count,),
            in_specs=[pl.BlockSpec((ZL, rows, TOKENS), lambda i, f: (0, 0, 0), pipeline_mode=pl.Buffered(1))] * (2 * RING)
            + [pl.BlockSpec((2 * TOKENS, width), lambda i, f: (0, lax.rem(f[0] + i, RING)))] * RING,
            out_specs=[pl.BlockSpec(chunk, lambda i, f: (0, 0, 0), pipeline_mode=pl.Buffered(1))] * count,
        ),
        out_shape=[jax.ShapeDtypeStruct(chunk, BF)] * count,
        compiler_params=params(PRODUCT_MIB),
        cost_estimate=pl.CostEstimate(flops=2 * ZL * rows * 1024 * width * count, bytes_accessed=2**21 * (1 + count), transcendentals=0),
        name="product",
    )(first, *outs, *ws)


def shards(queries, keys, values, head_grads, cotangent, old, new, doc_lengths):
    here = lax.axis_index(FLAT).astype(jnp.int32)
    lengths = doc_lengths.reshape(1, -1)
    old = old.reshape(1, -1)
    new = new.reshape(1, -1)
    core, x, y = (lax.axis_index(a).astype(jnp.int32) for a in ("core", "x", "y"))
    in_group = jnp.where(core == 0, y, x)
    in_reduce = jnp.where(core == 0, x, y)
    place = jnp.stack([here, in_group, in_reduce, core])

    kv, keep, send = prepare(place, old, new, keys, values, cotangent)
    kvs = from_predecessors(kv, y) + [kv]
    w_mine = jnp.concatenate([keep, core_swap(send)], axis=0)
    kvs[AFTER], w_soon = lax.optimization_barrier((kvs[AFTER], w_mine))
    *kvs, w_late = lax.optimization_barrier((*kvs, w_mine))
    ws = [w_mine] + [group_turn(w_soon if by == 2 else w_late, by) for by in range(1, RING)]

    same, cross, logs = attention_forward(place, lengths, queries, kvs)
    dq, own, *backs = attention_backward(place, lengths, old, new, queries, head_grads, logs, kvs)
    pieces = [*same, *cross]
    pieces[2] = group_turn(same[2], 2)
    pieces[RING + 2] = cross_turn(cross[2], 2)
    *pieces, ws[1], ws[2], ws[3], own = lax.optimization_barrier((*pieces, *ws[1:], own))
    same, cross = pieces[:RING], pieces[RING:]
    outs = []
    for by in range(RING):
        outs.append(group_turn(same[by], by) if by % 2 else same[by])
        outs.append(cross[by] if by == 2 else cross_turn(cross[by], by))

    first = ((in_reduce + 1) % RING).reshape(1)
    sent = product(first, RING - 1, outs, ws)
    got = [reduce_turn(part, by) for by, part in enumerate(sent, 1)]

    (mine,) = product(in_reduce.reshape(1), 1, outs, ws)
    part = sum((g.astype(F32) for g in got), mine.astype(F32)).astype(BF)
    dkv = brought_home(own, backs, y)
    dkv, part = lax.optimization_barrier((dkv, part))
    part = lax.all_to_all(part, ("zh", "zl"), split_axis=0, concat_axis=0, tiled=True)
    total = jnp.sum(part.astype(F32), axis=0).astype(BF)

    grad_weight = jnp.where((core == 1) & (x != y), transposed(total), total).astype(F32)
    return dq, dkv[0], dkv[1], grad_weight


def solution(mesh):
    mesh = Mesh(mesh.devices.reshape(ZH, RING, 2, ZL, RING), FLAT)
    tokens = P(FLAT, None)
    return jax.shard_map(
        shards,
        mesh=mesh,
        in_specs=(tokens, tokens, tokens, tokens, tokens, P(FLAT), P(FLAT), P()),
        out_specs=(tokens, tokens, tokens, P(("zl", "y"), ("zh", "x", "core"))),
        check_vma=False,
    )
```

```python
import itertools
import math

import jax
import jax.numpy as jnp
from jax import lax
from jax.experimental import pallas as pl
from jax.experimental.pallas import tpu as pltpu
from jax.sharding import Mesh, PartitionSpec as P

HEAD = 128
TOKENS = 128
BACK = 4
SPAN = (BACK + 1) * TOKENS
KV_HEADS = 4
GROUP = 8
HEADS_AT_ONCE = 8
ZH, ZL, RING = 4, 2, 4
ROWS = 1024
FORWARD_MIB, BACKWARD_MIB, PREPARE_MIB, PRODUCT_MIB = 28, 56, 12, 44
AFTER = 3
CLIP = 2.0
NEG = -1e30
SCALE = 1.0 / math.sqrt(HEAD)
LOG2E = math.log2(math.e)
FLAT = ("zh", "x", "core", "zl", "y")
BF = jnp.bfloat16
F32 = jnp.float32

NT = (((1,), (1,)), ((), ()))


def dot(a, b):
    return jnp.dot(a, b, preferred_element_type=F32)


def dot_nt(a, b):
    return lax.dot_general(a, b, NT, preferred_element_type=F32)


def mask_bias(here, lengths):
    row = lax.broadcasted_iota(jnp.int32, (TOKENS, TOKENS), 0)
    col = lax.broadcasted_iota(jnp.int32, (TOKENS, TOKENS), 1)
    lens = jnp.broadcast_to(lengths.astype(F32), (TOKENS, TOKENS))
    ends = jnp.sum(jnp.where(col <= row, lens, 0.0), axis=1, keepdims=True)
    lens_col = jnp.sum(jnp.where(col == row, lens, 0.0), axis=1, keepdims=True)
    base = here * TOKENS
    pos = (base + col).astype(F32)
    first = jnp.sum(jnp.where(ends <= pos, lens_col, 0.0), axis=0, keepdims=True)
    first = first.astype(jnp.int32)
    key = base - BACK * TOKENS + lax.broadcasted_iota(jnp.int32, (SPAN, TOKENS), 0)
    query = base + lax.broadcasted_iota(jnp.int32, (SPAN, TOKENS), 1)
    seen = (key <= query) & (key >= first)
    return jnp.where(seen, 0.0, NEG)


def scores_of(keys, q_pair, bias):
    return dot_nt(keys, q_pair) * (SCALE * LOG2E) + bias


def rows_of_heads(ref, at, count):
    return jnp.concatenate([ref[:, h * HEAD : (h + 1) * HEAD] for h in range(at, at + count)], axis=0)


def forward_kernel(here_ref, len_ref, q_ref, *refs):
    kv_refs = refs[: BACK + 1]
    own_refs = refs[BACK + 1 : BACK + 1 + RING]
    cross_refs = refs[BACK + 1 + RING : BACK + 1 + 2 * RING]
    log_ref, bias_ref = refs[BACK + 1 + 2 * RING :]
    g = pl.program_id(0)

    @pl.when(g == 0)
    def _():
        bias_ref[...] = mask_bias(here_ref[0], len_ref[...])

    keys = jnp.concatenate([r[0] for r in kv_refs], axis=0)
    values_t = jnp.concatenate([r[1] for r in kv_refs], axis=0).T
    bias = jnp.concatenate([bias_ref[...]] * HEADS_AT_ONCE, axis=1)
    zl = g // 2
    quads = []
    for at in range(0, GROUP, HEADS_AT_ONCE):
        s = scores_of(keys, rows_of_heads(q_ref, at, HEADS_AT_ONCE), bias)
        top = jnp.max(s, axis=0, keepdims=True)
        p = jnp.exp2(s - top)
        total = jnp.sum(p, axis=0, keepdims=True)
        out_t = (dot(values_t, p.astype(BF)) / total).astype(BF)
        log_total = top + jnp.log2(total)
        for i in range(HEADS_AT_ONCE):
            h = at + i
            quads.append(out_t[:, i * TOKENS : (i + 1) * TOKENS])
            log_ref[0, h : h + 1, :] = log_total[:, i * TOKENS : (i + 1) * TOKENS]
    for u in range(2):
        quad = jnp.concatenate(quads[4 * u : 4 * u + 4], axis=0)
        row_group = lax.rem(2 * g + u, RING)
        for group, out_refs in ((here_ref[1], own_refs), (here_ref[2], cross_refs)):
            away = lax.rem(row_group - group + RING, RING)
            for k, ref in enumerate(out_refs):

                @pl.when(away == k)
                def _(ref=ref, quad=quad):
                    ref[zl] = quad


def column_of(row):
    r = lax.broadcasted_iota(jnp.int32, (TOKENS, TOKENS), 0)
    c = lax.broadcasted_iota(jnp.int32, (TOKENS, TOKENS), 1)
    return jnp.sum(jnp.where(r == c, jnp.broadcast_to(row, (TOKENS, TOKENS)), 0.0), axis=1, keepdims=True)


def ratio_column(old_ref, new_ref):
    return column_of(jnp.minimum(jnp.exp(new_ref[...] - old_ref[...]), CLIP))


def backward_kernel(here_ref, len_ref, old_ref, new_ref, q_ref, g_ref, log_ref, *refs):
    kv_refs = refs[: BACK + 1]
    dq_ref, own_ref = refs[BACK + 1 : BACK + 3]
    back_refs = refs[BACK + 3 : 2 * BACK + 3]
    bias_ref, ratio_ref = refs[2 * BACK + 3 :]

    @pl.when(pl.program_id(0) == 0)
    def _():
        bias_ref[...] = mask_bias(here_ref[0], len_ref[...])
        ratio_ref[...] = jnp.broadcast_to(ratio_column(old_ref, new_ref), (TOKENS, HEAD))

    keys = jnp.concatenate([r[0] for r in kv_refs], axis=0)
    values = jnp.concatenate([r[1] for r in kv_refs], axis=0)
    keys_t = keys.T
    bias = jnp.concatenate([bias_ref[...]] * HEADS_AT_ONCE, axis=1)
    ratio = jnp.concatenate([ratio_ref[...]] * HEADS_AT_ONCE, axis=0)
    dk = jnp.zeros((SPAN, HEAD), F32)
    dv = jnp.zeros((SPAN, HEAD), F32)
    for at in range(0, GROUP, HEADS_AT_ONCE):
        q = rows_of_heads(q_ref, at, HEADS_AT_ONCE)
        grad = (rows_of_heads(g_ref, at, HEADS_AT_ONCE).astype(F32) * ratio).astype(BF)
        logs = jnp.concatenate([log_ref[0, h : h + 1, :] for h in range(at, at + HEADS_AT_ONCE)], axis=1)
        p = jnp.exp2(scores_of(keys, q, bias) - logs)
        dp = dot_nt(values, grad)
        delta = jnp.sum(p * dp, axis=0, keepdims=True)
        ds = (p * (dp - delta)).astype(BF)
        dv = dv + dot(p.astype(BF), grad)
        dk = dk + dot(ds, q)
        dq_t = dot(keys_t, ds) * SCALE
        for i in range(HEADS_AT_ONCE):
            h = at + i
            dq_ref[:, h * HEAD : (h + 1) * HEAD] = dq_t[:, i * TOKENS : (i + 1) * TOKENS].T
    dk = dk * SCALE
    own_ref[0] = dk[BACK * TOKENS :]
    own_ref[1] = dv[BACK * TOKENS :]
    for j, ref in enumerate(back_refs):
        at = (BACK - 1 - j) * TOKENS
        ref[0] = dk[at : at + TOKENS].astype(BF)
        ref[1] = dv[at : at + TOKENS].astype(BF)


def params(mib):
    return pltpu.CompilerParams(vmem_limit_bytes=mib * 2**20)


KV_SPEC = pl.BlockSpec((2, TOKENS, HEAD), lambda g, *_: (0, 0, g))
ROW_SPEC = pl.BlockSpec((1, TOKENS), lambda g, *_: (0, 0))
Q_SPEC = pl.BlockSpec((TOKENS, GROUP * HEAD), lambda g, *_: (0, g))
LOG_SPEC = pl.BlockSpec((1, GROUP, TOKENS), lambda g, *_: (g, 0, 0))


def attention_forward(place, lengths, q, kvs):
    piece = (ZL, ROWS // ZL, TOKENS)
    out = pl.pallas_call(
        forward_kernel,
        grid_spec=pltpu.PrefetchScalarGridSpec(
            num_scalar_prefetch=1,
            grid=(KV_HEADS,),
            in_specs=[ROW_SPEC, Q_SPEC] + [KV_SPEC] * (BACK + 1),
            out_specs=[pl.BlockSpec(piece, lambda g, *_: (0, 0, 0))] * (2 * RING) + [LOG_SPEC],
            scratch_shapes=[pltpu.VMEM((SPAN, TOKENS), F32)],
        ),
        out_shape=[jax.ShapeDtypeStruct(piece, BF)] * (2 * RING)
        + [jax.ShapeDtypeStruct((KV_HEADS, GROUP, TOKENS), F32)],
        compiler_params=params(FORWARD_MIB),
        cost_estimate=pl.CostEstimate(flops=2 * 2 * 32 * 128 * 640 * 128, bytes_accessed=2**22, transcendentals=32 * 128 * 640),
        name="attention_forward",
    )(place, lengths, q, *kvs)
    return out[:RING], out[RING : 2 * RING], out[2 * RING]


def attention_backward(here, lengths, old, new, q, g, logs, kvs):
    kv_shape = (2, TOKENS, KV_HEADS * HEAD)
    return pl.pallas_call(
        backward_kernel,
        grid_spec=pltpu.PrefetchScalarGridSpec(
            num_scalar_prefetch=1,
            grid=(KV_HEADS,),
            in_specs=[ROW_SPEC, ROW_SPEC, ROW_SPEC, Q_SPEC, Q_SPEC, LOG_SPEC] + [KV_SPEC] * (BACK + 1),
            out_specs=[Q_SPEC, KV_SPEC] + [KV_SPEC] * BACK,
            scratch_shapes=[pltpu.VMEM((SPAN, TOKENS), F32), pltpu.VMEM((TOKENS, HEAD), F32)],
        ),
        out_shape=[
            jax.ShapeDtypeStruct(q.shape, F32),
            jax.ShapeDtypeStruct(kv_shape, F32),
        ]
        + [jax.ShapeDtypeStruct(kv_shape, BF)] * BACK,
        compiler_params=params(BACKWARD_MIB),
        cost_estimate=pl.CostEstimate(flops=5 * 2 * 32 * 128 * 640 * 128, bytes_accessed=2**23, transcendentals=32 * 128 * 640),
        name="attention_backward",
    )(here, lengths, old, new, q, g, logs, *kvs)


def along_tokens(v, by):
    count = math.prod(lax.axis_size(axis) for axis in FLAT)
    return lax.ppermute(v, FLAT, [(i, i + by) for i in range(count) if 0 <= i + by < count])


def moved(v, to):
    sizes = [lax.axis_size(axis) for axis in FLAT]
    pairs = []
    for i, at in enumerate(itertools.product(*map(range, sizes))):
        there = to(*at)
        if there is not None:
            pairs.append((i, sum(c * math.prod(sizes[j + 1 :]) for j, c in enumerate(there))))
    return lax.ppermute(v, FLAT, pairs)


def core_swap(v):
    return moved(v, lambda zh, x, c, zl, y: (zh, x, 1 - c, zl, y))


def group_turn(v, by):
    return moved(v, lambda zh, x, c, zl, y: (zh, (x + by * c) % RING, c, zl, (y + by * (1 - c)) % RING))


def cross_turn(v, by):
    return moved(v, lambda zh, x, c, zl, y: (zh, (x + by * (1 - c)) % RING, 1 - c, zl, (y + by * c) % RING))


def reduce_turn(v, by):
    return moved(v, lambda zh, x, c, zl, y: (zh, (x + by * (1 - c)) % RING, c, zl, (y + by * c) % RING))


def transposed(v):
    return moved(v, lambda zh, x, c, zl, y: (zh, y, c, zl, x) if c == 1 and x != y else None)


def y_turn(v, by):
    return moved(v, lambda zh, x, c, zl, y: (zh, x, c, zl, (y + by) % RING))


def from_predecessors(kv, y):
    before = along_tokens(kv, BACK)
    return [before] + [y_turn(jnp.where(y + by < RING, kv, before), by) for by in range(BACK - 1, 0, -1)]


def brought_home(own, backs, y):
    before = backs[RING - 1].astype(F32)
    for by in range(1, RING):
        part = moved(backs[by - 1], lambda zh, x, c, zl, y: (zh, x, c, zl, (y - by) % RING)).astype(F32)
        here = y + by < RING
        own = own + jnp.where(here, part, 0.0)
        before = before + jnp.where(here, 0.0, part)
    return own + along_tokens(before.astype(BF), -RING).astype(F32)


def prepare_kernel(place_ref, old_ref, new_ref, cot_ref, keep_ref, send_ref):
    ratio = ratio_column(old_ref, new_ref)
    core = place_ref[3]
    for out_ref, half in ((keep_ref, core), (send_ref, 1 - core)):
        for chunk in range(RING):
            for zh in range(ZH):
                at = pl.multiple_of((zh * 2 * RING + chunk * 2 + half) * HEAD, HEAD)
                to = (chunk * ZH + zh) * HEAD
                part = cot_ref[:, pl.ds(at, HEAD)].astype(F32) * ratio
                out_ref[:, to : to + HEAD] = part.astype(BF)


def prepare(place, old, new, cotangent):
    half = jax.ShapeDtypeStruct((TOKENS, cotangent.shape[1] // 2), BF)
    smem = pl.BlockSpec(memory_space=pltpu.SMEM)
    vmem = pl.BlockSpec(memory_space=pltpu.VMEM)
    return pl.pallas_call(
        prepare_kernel,
        in_specs=[smem] + [vmem] * 3,
        out_specs=[vmem] * 2,
        out_shape=[half, half],
        compiler_params=params(PREPARE_MIB),
        cost_estimate=pl.CostEstimate(flops=2**20, bytes_accessed=2**22, transcendentals=0),
        name="prepare",
    )(place, old, new, cotangent)


def product_kernel(first_ref, *refs):
    o_refs, w_refs, out_refs = refs[: 2 * RING], refs[2 * RING : 3 * RING], refs[3 * RING :]
    rows = o_refs[0].shape[1]
    lhs = jnp.concatenate([r[...].reshape(ZL * rows, TOKENS) for r in o_refs], axis=1)
    rhs = jnp.concatenate([r[...] for r in w_refs], axis=0)
    part = dot(lhs, rhs).astype(BF)
    for step, ref in enumerate(out_refs):

        @pl.when(pl.program_id(0) == step)
        def _(ref=ref):
            for zh in range(ZH):
                for zl in range(ZL):
                    ref[zh * ZL + zl] = part[zl * rows : (zl + 1) * rows, zh * HEAD : (zh + 1) * HEAD]


def product(first, count, outs, ws):
    rows = ROWS // ZL
    chunk = (ZH * ZL, rows, HEAD)
    width = ZH * HEAD
    return pl.pallas_call(
        product_kernel,
        grid_spec=pltpu.PrefetchScalarGridSpec(
            num_scalar_prefetch=1,
            grid=(count,),
            in_specs=[pl.BlockSpec((ZL, rows, TOKENS), lambda i, f: (0, 0, 0), pipeline_mode=pl.Buffered(1))] * (2 * RING)
            + [pl.BlockSpec((2 * TOKENS, width), lambda i, f: (0, lax.rem(f[0] + i, RING)))] * RING,
            out_specs=[pl.BlockSpec(chunk, lambda i, f: (0, 0, 0), pipeline_mode=pl.Buffered(1))] * count,
        ),
        out_shape=[jax.ShapeDtypeStruct(chunk, BF)] * count,
        compiler_params=params(PRODUCT_MIB),
        cost_estimate=pl.CostEstimate(flops=2 * ZL * rows * 1024 * width * count, bytes_accessed=2**21 * (1 + count), transcendentals=0),
        name="product",
    )(first, *outs, *ws)


def shards(queries, keys, values, head_grads, cotangent, old, new, doc_lengths):
    here = lax.axis_index(FLAT).astype(jnp.int32)
    lengths = doc_lengths.reshape(1, -1)
    old = old.reshape(1, -1)
    new = new.reshape(1, -1)
    core, x, y = (lax.axis_index(a).astype(jnp.int32) for a in ("core", "x", "y"))
    in_group = jnp.where(core == 0, y, x)
    in_reduce = jnp.where(core == 0, x, y)
    place = jnp.stack([here, in_group, in_reduce, core])

    kv = jnp.stack([keys, values])
    kv, prepare_place = lax.optimization_barrier((kv, place))
    keep, send = prepare(prepare_place, old, new, cotangent)
    kvs = from_predecessors(kv, y) + [kv]
    w_mine = jnp.concatenate([keep, core_swap(send)], axis=0)
    w_soon = w_mine
    *kvs, w_late = lax.optimization_barrier((*kvs, w_mine))
    ws = [w_mine] + [group_turn(w_soon if by == 2 else w_late, by) for by in range(1, RING)]

    same, cross, logs = attention_forward(place, lengths, queries, kvs)
    dq, own, *backs = attention_backward(place, lengths, old, new, queries, head_grads, logs, kvs)
    pieces = [*same, *cross]
    pieces[RING] = cross_turn(cross[0], 0)
    pieces[RING + 2] = cross_turn(cross[2], 2)
    *pieces, ws[1], ws[2], ws[3], own = lax.optimization_barrier((*pieces, *ws[1:], own))
    same, cross = pieces[:RING], pieces[RING:]
    outs = []
    for by in range(RING):
        outs.append(same[by] if by in (0,) else group_turn(same[by], by))
        outs.append(cross[by] if by in (0, 2) else cross_turn(cross[by], by))

    first = ((in_reduce + 1) % RING).reshape(1)
    sent = product(first, RING - 1, outs, ws)
    got = [reduce_turn(part, by) for by, part in enumerate(sent, 1)]

    (mine,) = product(in_reduce.reshape(1), 1, outs, ws)
    part = sum((g.astype(F32) for g in got), mine.astype(F32)).astype(BF)
    dkv = brought_home(own, backs, y)
    dkv, part = lax.optimization_barrier((dkv, part))
    part = lax.all_to_all(part, ("zh", "zl"), split_axis=0, concat_axis=0, tiled=True)
    total = jnp.sum(part.astype(F32), axis=0).astype(BF)

    grad_weight = jnp.where((core == 1) & (x != y), transposed(total), total).astype(F32)
    return dq, dkv[0], dkv[1], grad_weight


def solution(mesh):
    mesh = Mesh(mesh.devices.reshape(ZH, RING, 2, ZL, RING), FLAT)
    tokens = P(FLAT, None)
    return jax.shard_map(
        shards,
        mesh=mesh,
        in_specs=(tokens, tokens, tokens, tokens, tokens, P(FLAT), P(FLAT), P()),
        out_specs=(tokens, tokens, tokens, P(("zl", "y"), ("zh", "x", "core"))),
        check_vma=False,
    )
```
